32 devices in a mesh: groups: 2 (over y), zone: 4 (over x, core), tile: 4 (over z).
Axes of the slice: x: 2, y: 2, z: 4, core: 2. Of those that a mesh axis runs over, the one named last changes fastest.
Arguments:
- backscatter: bfloat16 [8, 2, 256, 512], P(('groups', 'zone'), None, 'tile'), parts along dimension 0, may hold values from -6 to 6
- row_bank: bfloat16 [16, 128, 128], replicated, may hold values from -0.3125 to 0.3125
- row_index: int32 [8, 4, 3], P(('groups', 'zone')), parts along dimension 0, may hold values from 0 to 3
- row_pick: int32 [8, 4, 3], P(('groups', 'zone')), parts along dimension 0, may hold values from 0 to 15
- row_mask: int32 [8, 4, 3], P(('groups', 'zone')), parts along dimension 0, may hold values 0 or 1
- column_bank: bfloat16 [16, 128, 128], replicated, may hold values from -0.3125 to 0.3125
- column_index: int32 [8, 2, 3], P(('groups', 'zone')), parts along dimension 0, may hold values from 0 to 1
- column_pick: int32 [8, 2, 3], P(('groups', 'zone')), parts along dimension 0, may hold values from 0 to 15
- column_mask: int32 [8, 2, 3], P(('groups', 'zone')), parts along dimension 0, may hold values 0 or 1
Outputs:
- geocoded: bfloat16 [8, 2, 256, 512], P(('groups', 'zone'), None, None, 'tile'), parts along dimension 0
The draws below stay inside these ranges and needn't reach their ends.
There are 2 independent parts, one for each index of `groups`. The reference program is written for one: setup_inputs(seed, part) draws one part's arguments, and reference() takes and returns one part's arrays. A program takes and returns all parts, laid end to end along the dimension named above; an argument that names none is the same for every part. Nothing has to cross between parts.
All inputs are finite; a program needn't handle non-finite values. No bound on the sum of `row_mask` or of `column_mask` on one device may be relied on, other than what follows from the above.
Results may differ from the reference program's by a relative error of at most 0.0049.
Values may be sent and summed in bfloat16 or wider, within the bound.
A program may use at most 64 MiB of HBM per device.

```python
import jax
import jax.numpy as jnp
from jax import lax

BLOCK = 128
EDGE = 64
NBANK = 16
ZONES = 4
LINES = 256
ROWS = 256
SAMPLES = 512
COLUMN_BLOCKS = 4
LINE_BLOCKS = 2


def place_ends(drawn, rng, low, largest):
    spot = [jax.random.randint(jax.random.fold_in(rng, axis), (), 0, length) for axis, length in enumerate(drawn.shape)]
    longest = drawn.shape.index(max(drawn.shape))
    neighbour = spot[:longest] + [(spot[longest] + 1) % drawn.shape[longest]] + spot[longest + 1:]
    return drawn.at[tuple(spot)].set(low).at[tuple(neighbour)].set(largest)


def steps_of(own_key, dims, shards, least, high):
    factor_of = 1.0
    for position, parts in shards:
        heights = jax.random.uniform(jax.random.fold_in(jax.random.fold_in(own_key, 6), position), (parts,), jnp.float32, least / len(shards), high / len(shards))
        factor_of = factor_of * jnp.repeat(jnp.exp(heights), dims[position] // parts).reshape((-1,) + (1,) * (len(dims) - 1 - position))
    return factor_of


def normal_values(own_key, dims, width, bound, cuts=(), held_as=jnp.bfloat16):
    entries = jax.random.normal(own_key, dims, jnp.float32) * width
    if len(cuts) > 0:
        entries = steps_of(own_key, dims, cuts, -0.22, 0.18) * entries
    return jnp.clip(entries, min=-bound, max=bound).astype(held_as)


def setup_inputs(seed: int = 0, part: int = 0) -> dict:
    arg_keys = jax.random.split(jax.random.key(seed), 10)
    part_keys = jax.random.split(jax.random.fold_in(arg_keys[9], part), 10)
    return {
        "backscatter": normal_values(part_keys[0], (ZONES, 2, LINES, SAMPLES), 1.0, 6.0, ((0, 4), (2, 4))),
        "row_bank": normal_values(arg_keys[1], (NBANK, BLOCK, BLOCK), (3 * BLOCK) ** -0.5, 0.3125),
        "row_index": place_ends(jax.random.randint(part_keys[2], (ZONES, COLUMN_BLOCKS, 3), 0, COLUMN_BLOCKS), jax.random.fold_in(part_keys[2], 1), 0, COLUMN_BLOCKS - 1).astype(jnp.int32),
        "row_pick": place_ends(jax.random.randint(part_keys[3], (ZONES, COLUMN_BLOCKS, 3), 0, NBANK), jax.random.fold_in(part_keys[3], 1), 0, NBANK - 1).astype(jnp.int32),
        "row_mask": place_ends((jax.random.randint(part_keys[4], (ZONES, COLUMN_BLOCKS, 3), 0, 4) < 3).astype(jnp.int32), jax.random.fold_in(part_keys[4], 1), 0, 1),
        "column_bank": normal_values(arg_keys[5], (NBANK, BLOCK, BLOCK), (3 * BLOCK) ** -0.5, 0.3125),
        "column_index": place_ends(jax.random.randint(part_keys[6], (ZONES, LINE_BLOCKS, 3), 0, LINE_BLOCKS), jax.random.fold_in(part_keys[6], 1), 0, LINE_BLOCKS - 1).astype(jnp.int32),
        "column_pick": place_ends(jax.random.randint(part_keys[7], (ZONES, LINE_BLOCKS, 3), 0, NBANK), jax.random.fold_in(part_keys[7], 1), 0, NBANK - 1).astype(jnp.int32),
        "column_mask": place_ends((jax.random.randint(part_keys[8], (ZONES, LINE_BLOCKS, 3), 0, 4) < 3).astype(jnp.int32), jax.random.fold_in(part_keys[8], 1), 0, 1),
    }


def resample_rows(image, index, pick, mask, row_bank):
    blocks = image.reshape(2, LINES, COLUMN_BLOCKS, BLOCK)

    def per_block(item):
        band_index, band_pick, band_mask = item
        gathered = blocks[:, :, band_index, :].astype(jnp.float32)
        weights = row_bank[band_pick].astype(jnp.float32) * band_mask.astype(jnp.float32)[:, None, None]
        return jnp.einsum("clbi,bij->clj", gathered, weights).astype(jnp.bfloat16)

    stacked = lax.map(per_block, (index, pick, mask))
    return jnp.transpose(stacked, (1, 2, 0, 3)).reshape(2, LINES, SAMPLES)


def resample_columns(image, index, pick, mask, column_bank):
    blocks = image.reshape(2, LINE_BLOCKS, BLOCK, SAMPLES)

    def per_block(item):
        band_index, band_pick, band_mask = item
        gathered = blocks[:, band_index].astype(jnp.float32)
        weights = column_bank[band_pick].astype(jnp.float32) * band_mask.astype(jnp.float32)[:, None, None]
        return jnp.einsum("cbik,boi->cok", gathered, weights).astype(jnp.bfloat16)

    stacked = lax.map(per_block, (index, pick, mask))
    return jnp.transpose(stacked, (1, 0, 2, 3)).reshape(2, ROWS, SAMPLES)


def reference(backscatter, row_bank, row_index, row_pick, row_mask, column_bank, column_index, column_pick, column_mask):
    def per_zone(entry):
        image, rindex, rpick, rmask, cindex, cpick, cmask = entry
        along_samples = resample_rows(image, rindex, rpick, rmask, row_bank)
        return resample_columns(along_samples, cindex, cpick, cmask, column_bank)

    gridded = lax.map(per_zone, (backscatter, row_index, row_pick, row_mask, column_index, column_pick, column_mask))
    feather = ((jnp.arange(EDGE, dtype=jnp.float32) + 0.5) / EDGE)[:, None]
    bottoms = gridded[:-1, :, ROWS - EDGE:, :].astype(jnp.float32)
    tops = gridded[1:, :, :EDGE, :].astype(jnp.float32)
    blended = ((1.0 - feather) * bottoms + feather * tops).astype(jnp.bfloat16)
    gridded = gridded.at[:-1, :, ROWS - EDGE:, :].set(blended)
    gridded = gridded.at[1:, :, :EDGE, :].set(blended)
    return gridded
```

```python
import functools

import jax
import jax.numpy as jnp
from jax import lax
from jax.experimental import pallas as pl
from jax.experimental.pallas import tpu as pltpu
from jax.sharding import PartitionSpec as P

BLOCK = 128
EDGE = 64
MESH = pl.DeviceIdType.MESH


def repeat(count, body):
    if count <= 8:
        for i in range(count):
            body(i)
    else:
        lax.fori_loop(0, count, lambda i, c: (body(i), c)[1], 0)


def kernel(
    tiles,
    zones,
    image_hbm,
    row_bank_hbm,
    row_index_hbm,
    row_pick_hbm,
    row_mask_hbm,
    column_bank_hbm,
    column_index_hbm,
    column_pick_hbm,
    column_mask_hbm,
    out_hbm,
    image,
    row_bank,
    row_index,
    row_pick,
    row_mask,
    column_bank,
    column_index,
    column_pick,
    column_mask,
    stage,
    held,
    panels,
    arrived,
    out,
    load_sem,
    image_sem,
    send_sem,
    recv_sem,
    edge_send_sem,
    edge_recv_sem,
    store_sem,
):
    me = lax.axis_index("tile")
    zone = lax.axis_index("zone")
    sample_blocks, channels, lines, _ = image.shape
    pieces, piece, _ = stage.shape[1:]
    bank = row_bank_hbm.shape[0]
    bands = row_index.shape[0]
    own_blocks = row_index.shape[2] // tiles
    width = own_blocks * BLOCK
    line_blocks = column_index.shape[1]
    rows = line_blocks * BLOCK

    loads = [
        pltpu.make_async_copy(source, target, load_sem.at[i])
        for i, (source, target) in enumerate(
            (
                (row_index_hbm, row_index),
                (row_pick_hbm, row_pick),
                (row_mask_hbm, row_mask),
                (row_bank_hbm, row_bank.at[pl.ds(0, bank)]),
                (column_index_hbm, column_index),
                (column_pick_hbm, column_pick),
                (column_mask_hbm, column_mask),
                (column_bank_hbm, column_bank.at[pl.ds(0, bank)]),
            )
        )
    ]

    def image_load(i):
        start = i * BLOCK if isinstance(i, int) else pl.multiple_of(i * BLOCK, BLOCK)
        return pltpu.make_async_copy(
            image_hbm.at[0, :, :, pl.ds(start, BLOCK)], image.at[i], image_sem.at[i]
        )

    for load in loads[:3]:
        load.start()
    repeat(sample_blocks, lambda i: image_load(i).start())
    for load in loads[3:]:
        load.start()

    barrier = pltpu.get_barrier_semaphore()

    def greet(i):
        pl.semaphore_signal(
            barrier, inc=1, device_id={"tile": lax.rem(me + i + 1, tiles)}, device_id_type=MESH
        )

    repeat(tiles - 1, greet)

    @pl.when(zone > 0)
    def _():
        pl.semaphore_signal(barrier, inc=1, device_id={"zone": zone - 1}, device_id_type=MESH)

    @pl.when(zone < zones - 1)
    def _():
        pl.semaphore_signal(barrier, inc=1, device_id={"zone": zone + 1}, device_id_type=MESH)

    zero = jnp.zeros((BLOCK, BLOCK), jnp.bfloat16)
    row_bank[bank] = zero
    column_bank[bank] = zero

    for load in loads[:4]:
        load.wait()
    repeat(sample_blocks, lambda i: image_load(i).wait())

    def resampled(column_block):
        parts, kernels = [], []
        for b in range(bands):
            part = image[row_index[b, 0, column_block]]
            parts.append(part.reshape(channels * lines, BLOCK))
            valid = row_mask[b, 0, column_block]
            kernels.append(row_bank[valid * row_pick[b, 0, column_block] + (1 - valid) * bank])
        product = jnp.dot(
            jnp.concatenate(parts, axis=1),
            jnp.concatenate(kernels, axis=0),
            preferred_element_type=jnp.float32,
        )
        return product.astype(jnp.bfloat16)

    def fill(target, tile):
        for j in range(own_blocks):
            block = resampled(tile * own_blocks + j)
            for c in range(channels):
                for p in range(pieces):
                    first = c * lines + p * piece
                    target[p, :, c * width + j * BLOCK : c * width + (j + 1) * BLOCK] = block[
                        first : first + piece
                    ]

    my_lines = pl.ds(me * pieces, pieces)

    def passage(slot, tile):
        return pltpu.make_async_remote_copy(
            src_ref=stage.at[slot],
            dst_ref=held.at[my_lines],
            send_sem=send_sem.at[slot],
            recv_sem=recv_sem.at[me],
            device_id={"tile": tile},
            device_id_type=MESH,
        )

    def offset(i):
        step = tiles // 2 + i
        return jnp.where(step >= tiles, step - tiles + 1, step) if not isinstance(step, int) else (
            step - tiles + 1 if step >= tiles else step
        )

    def send(i):
        tile = lax.rem(me + offset(i), tiles)
        fill(stage.at[i], tile)
        if isinstance(i, int) and i == 0:
            await_greetings()
        passage(i, tile).start()

    def await_greetings():
        @pl.when(zone == 0)
        def _():
            pl.semaphore_wait(barrier, tiles - 1 + (zones > 1))

        @pl.when(zone > 0)
        def _():
            @pl.when(zone < zones - 1)
            def _():
                pl.semaphore_wait(barrier, tiles + 1)

            @pl.when(zone == zones - 1)
            def _():
                pl.semaphore_wait(barrier, tiles)

    if tiles - 1 > 8:
        await_greetings()
    repeat(tiles - 1, send)
    fill(held.at[my_lines], me)

    for load in loads[4:]:
        load.wait()

    def arrival(i):
        tile = lax.rem(me + i + 1, tiles)
        theirs = pl.ds(tile * pieces, pieces)
        pltpu.make_async_remote_copy(
            src_ref=stage.at[i],
            dst_ref=held.at[theirs],
            send_sem=send_sem.at[i],
            recv_sem=recv_sem.at[tile],
            device_id={"tile": tile},
            device_id_type=MESH,
        ).wait_recv()

    repeat(tiles - 1, arrival)

    def gridded(r):
        parts, kernels = [], []
        for b in range(bands):
            for p in range(BLOCK // piece):
                parts.append(held[column_index[0, r, b] * (BLOCK // piece) + p])
            valid = column_mask[0, r, b]
            kernels.append(column_bank[valid * column_pick[0, r, b] + (1 - valid) * bank])
        product = jnp.dot(
            jnp.concatenate(kernels, axis=1),
            jnp.concatenate(parts, axis=0),
            preferred_element_type=jnp.float32,
        )
        return product.astype(jnp.bfloat16)

    def keep(block, row, row_count, first):
        for c in range(channels):
            out[0, c, pl.ds(first, row_count), :] = block[
                row : row + row_count, c * width : (c + 1) * width
            ]

    def handover(side, neighbour):
        return pltpu.make_async_remote_copy(
            src_ref=panels.at[side],
            dst_ref=arrived.at[side],
            send_sem=edge_send_sem.at[side],
            recv_sem=edge_recv_sem.at[side],
            device_id={"zone": neighbour},
            device_id_type=MESH,
        )

    top_to = zone - 1
    bottom_to = zone + 1
    last = line_blocks - 1
    block = gridded(0)
    panels[0] = block[:EDGE]

    @pl.when(zone > 0)
    def _():
        handover(0, top_to).start()

    if last > 0:
        keep(block, EDGE, BLOCK - EDGE, EDGE)
        block = gridded(last)
    panels[1] = block[BLOCK - EDGE :]

    @pl.when(zone < zones - 1)
    def _():
        handover(1, bottom_to).start()

    if last > 0:
        keep(block, 0, BLOCK - EDGE, last * BLOCK)
    if last > 1:

        def middle(i):
            keep(gridded(i + 1), 0, BLOCK, pl.multiple_of((i + 1) * BLOCK, BLOCK))

        repeat(last - 1, middle)

    def stored(i, first, count):
        return pltpu.make_async_copy(
            out.at[:, :, pl.ds(first, count), :],
            out_hbm.at[:, :, pl.ds(first, count), :],
            store_sem.at[i],
        )

    inner = stored(2, EDGE, rows - 2 * EDGE)
    if rows > 2 * EDGE:
        inner.start()
    feather = (
        lax.broadcasted_iota(jnp.int32, (EDGE, channels * width), 0).astype(jnp.float32) + 0.5
    ) / EDGE

    def blend(lower, upper):
        return (
            (1.0 - feather) * lower.astype(jnp.float32) + feather * upper.astype(jnp.float32)
        ).astype(jnp.bfloat16)

    @pl.when(zone > 0)
    def _():
        handover(1, top_to).wait_recv()
        keep(blend(arrived[1], panels[0]), 0, EDGE, 0)

    @pl.when(zone == 0)
    def _():
        keep(panels[0], 0, EDGE, 0)

    top_store = stored(0, 0, EDGE)
    top_store.start()

    @pl.when(zone < zones - 1)
    def _():
        handover(0, bottom_to).wait_recv()
        keep(blend(panels[1], arrived[0]), 0, EDGE, rows - EDGE)

    @pl.when(zone == zones - 1)
    def _():
        keep(panels[1], 0, EDGE, rows - EDGE)

    bottom_store = stored(1, rows - EDGE, EDGE)
    bottom_store.start()

    def sent(i):
        passage(i, lax.rem(me + i + 1, tiles)).wait_send()

    repeat(tiles - 1, sent)

    @pl.when(zone > 0)
    def _():
        handover(0, top_to).wait_send()

    @pl.when(zone < zones - 1)
    def _():
        handover(1, bottom_to).wait_send()

    if rows > 2 * EDGE:
        inner.wait()
    top_store.wait()
    bottom_store.wait()


def solution(mesh):
    tiles = mesh.shape["tile"]
    zones = mesh.shape["zone"]

    def on_device(
        backscatter,
        row_bank,
        row_index,
        row_pick,
        row_mask,
        column_bank,
        column_index,
        column_pick,
        column_mask,
    ):
        _, channels, lines, samples = backscatter.shape
        bank = row_bank.shape[0]
        width = samples // tiles
        piece = min(lines, BLOCK)
        rows = column_index.shape[1] * BLOCK
        row_index, row_pick, row_mask = (
            jnp.transpose(table, (2, 0, 1)) for table in (row_index, row_pick, row_mask)
        )
        dma = pltpu.SemaphoreType.DMA
        return pl.pallas_call(
            functools.partial(kernel, tiles, zones),
            out_shape=jax.ShapeDtypeStruct((1, channels, rows, width), jnp.bfloat16),
            in_specs=[pl.BlockSpec(memory_space=pltpu.HBM)] * 9,
            out_specs=pl.BlockSpec(memory_space=pl.ANY),
            scratch_shapes=[
                pltpu.VMEM((samples // BLOCK, channels, lines, BLOCK), jnp.bfloat16),
                pltpu.VMEM((bank + 1, BLOCK, BLOCK), jnp.bfloat16),
                pltpu.SMEM(row_index.shape, jnp.int32),
                pltpu.SMEM(row_index.shape, jnp.int32),
                pltpu.SMEM(row_index.shape, jnp.int32),
                pltpu.VMEM((bank + 1, BLOCK, BLOCK), jnp.bfloat16),
                pltpu.SMEM(column_index.shape, jnp.int32),
                pltpu.SMEM(column_index.shape, jnp.int32),
                pltpu.SMEM(column_index.shape, jnp.int32),
                pltpu.VMEM((tiles - 1, lines // piece, piece, channels * width), jnp.bfloat16),
                pltpu.VMEM((tiles * lines // piece, piece, channels * width), jnp.bfloat16),
                pltpu.VMEM((2, EDGE, channels * width), jnp.bfloat16),
                pltpu.VMEM((2, EDGE, channels * width), jnp.bfloat16),
                pltpu.VMEM((1, channels, rows, width), jnp.bfloat16),
                dma((8,)),
                dma((samples // BLOCK,)),
                dma((tiles - 1,)),
                dma((tiles,)),
                dma((2,)),
                dma((2,)),
                dma((3,)),
            ],
            compiler_params=pltpu.CompilerParams(
                collective_id=0, has_side_effects=True, vmem_limit_bytes=48 * 2**20
            ),
        )(
            *(
                pltpu.with_memory_space_constraint(operand, pltpu.HBM)
                for operand in (
                    backscatter,
                    row_bank,
                    row_index,
                    row_pick,
                    row_mask,
                    column_bank,
                    column_index,
                    column_pick,
                    column_mask,
                )
            )
        )

    tables = P(("groups", "zone"), None, None)
    return jax.shard_map(
        on_device,
        mesh=mesh,
        in_specs=(
            P(("groups", "zone"), None, "tile", None),
            P(),
            tables,
            tables,
            tables,
            P(),
            tables,
            tables,
            tables,
        ),
        out_specs=P(("groups", "zone"), None, None, "tile"),
        check_vma=False,
    )
```
